32 devices in a mesh: groups: 2 (over y), ctx: 16 (over z, x, core).
Axes of the slice: x: 2, y: 2, z: 4, core: 2. Of those that a mesh axis runs over, the one named last changes fastest.
Arguments:
- inputs: bfloat16 [8192, 7168], P(('groups', 'ctx')), parts along dimension 0, may hold values from -6 to 6
- out_grads: bfloat16 [8192, 7168], P(('groups', 'ctx')), parts along dimension 0, may hold values from -6 to 6
- gates: float32 [8192, 8], P(('groups', 'ctx')), parts along dimension 0, may hold values from 0.05 to 0.8
- expert_ids: int32 [8192, 8], P(('groups', 'ctx')), parts along dimension 0, may hold values from 0 to 255, all different within a row; in each aligned block of 256 rows (0 to 255, 256 to 511, ...) at most 24 rows name the same one
- offsets: int32 [18], P('groups'), parts along dimension 0, may hold values from 0 to 4096, as said below
- projections: bfloat16 [7168, 128], replicated, may hold values from -0.0625 to 0.0625
Outputs:
- shared_sketch: float32 [16, 4096], P('groups', 'ctx'), parts along dimension 0
- routed_sketch: float32 [256, 16, 4096], P('ctx', 'groups'), parts along dimension 1
The draws below stay inside these ranges and needn't reach their ends.
There are 2 independent parts, one for each index of `groups`. The reference program is written for one: setup_inputs(seed, part) draws one part's arguments, and reference() takes and returns one part's arrays. A program takes and returns all parts, laid end to end along the dimension named above; an argument that names none is the same for every part. Nothing has to cross between parts.
Inputs may be any that keep to these rules, and one draw needn't show every extreme that they name: `expert_ids`: each row names 8 different experts. Within the 256 rows of one index of ctx no expert is named more than 24 times, and in every draw some expert is named exactly 24 times by the rows of some index. offsets[0] = 0, offsets[8] = 4096, strictly rising; every document holds more than 256 tokens.
All inputs are finite; a program needn't handle non-finite values.
Results may differ from the reference program's by a relative error of at most 0.0041.
Values may be sent and summed in bfloat16 or wider, within the bound.
No kernel may reach another device: no remote copies, remote signals or barrier semaphores. Data moves between devices by JAX's collectives and lax.ppermute only.
A program may use at most 128 MiB of HBM per device.

```python
import math
import jax
import jax.numpy as jnp
import numpy as np
from jax import lax

D = 7168
EXPERTS = 256
TOPK = 8
RANK = 64
DOCS = 8
TOK_DEV = 256
TOKENS = 4096
CAP = 24


def draw_offsets(key, part):
    key = jax.random.fold_in(key, 11)
    devices = TOKENS // TOK_DEV
    picks = jnp.sort(jax.random.randint(key, (DOCS - 1,), 0, devices - 2 * DOCS + 1))
    jitter = jax.random.randint(jax.random.fold_in(key, 1), (DOCS - 1,), 0, TOK_DEV)
    units = 2 * jnp.arange(1, DOCS, dtype=jnp.int32) + picks
    inner = units * TOK_DEV + jitter
    first = jnp.zeros((1,), jnp.int32)
    last = jnp.full((1,), TOKENS, jnp.int32)
    return jnp.concatenate([first, inner.astype(jnp.int32), last]).astype(jnp.int32)


def block_scale(own_key, extent, shards, smallest, high):
    def one(dim, parts):
        draws = jax.random.uniform(jax.random.fold_in(jax.random.fold_in(own_key, 6), dim), (parts,), jnp.float32, smallest / len(shards), high / len(shards))
        return jnp.repeat(jnp.exp(draws), extent[dim] // parts).reshape((-1,) + (1,) * (len(extent) - dim - 1))

    loudness = one(*shards[0])
    for cut in shards[1:]:
        loudness = loudness * one(*cut)
    return loudness


def assign_block(rng, own, number, rows, number_of, top, most, skew):
    sequence = jax.random.permutation(rng, number_of)
    packed, ordinary = portions_of(number_of, rows * top, most, skew, True), portions_of(number_of, rows * top, most, skew, False)
    places = jnp.arange(number_of)

    def named(sizes, rotation):
        used = int((sizes > 0).sum())
        fixed = max(1, used // 4)
        passed = fixed + (places - fixed + rotation * (used - fixed)) % max(1, number_of - fixed)
        return jnp.zeros((number_of,), jnp.int32).at[sequence[jnp.where(places < fixed, places, passed)]].set(jnp.asarray(sizes, jnp.int32))

    sizes = jnp.where(number % 4 == 0, named(packed, number // 4), named(ordinary, number - number // 4 - 1))
    mixed = jax.random.permutation(jax.random.fold_in(own, 3), number_of)
    giver, receiver = mixed[0:number_of // 2 * 2:2], mixed[1:number_of // 2 * 2:2]
    room = jnp.minimum(sizes[giver] - 1, most - sizes[receiver]) // 2
    room = jnp.where((giver == sequence[0]) | (receiver == sequence[0]) | (sizes[receiver] == 0), 0, jnp.maximum(room, 0))
    passed = jax.random.randint(jax.random.fold_in(own, 4), (number_of // 2,), 0, 1 << 20) % (room + 1)
    sizes = sizes.at[giver].add(-passed).at[receiver].add(passed)
    labels = jnp.searchsorted(jnp.cumsum(sizes), jnp.arange(rows * top), side="right").astype(jnp.int32)
    grid = labels.reshape(top, rows).T
    grid = grid[jax.random.permutation(jax.random.fold_in(own, 1), rows)]
    rotation = jax.random.randint(jax.random.fold_in(own, 2), (rows, 1), 0, top)
    return jnp.take_along_axis(grid, (jnp.arange(top)[None, :] + rotation) % top, axis=1)


def portions_of(count, total, bound, slope, full):
    weights = [(1 << 20) // math.isqrt(rank ** slope) + 1 for rank in range(1, count + 1)]
    largest = bound if full else min(bound, max(-(-total // count), total * weights[0] // sum(weights)))
    least = 1 if total - largest >= count - 1 else 0
    given, spare = [largest] + [least] * (count - 1), total - largest - least * (count - 1)
    while spare > 0:
        free = [i for i in range(1, count) if given[i] < largest] or [i for i in range(1, count) if given[i] < bound]
        mass, remaining = sum([weights[i] for i in free]), spare
        for i in free:
            extra = min(bound - given[i], max(1, remaining * weights[i] // mass), spare)
            given[i] = given[i] + extra
            spare = spare - extra
    return np.array(given)


def bell_draw(key, extent, scale, reach, cuts=(), kind=jnp.bfloat16):
    array = scale * jax.random.normal(key, extent, jnp.float32)
    if cuts:
        array = array * block_scale(key, extent, cuts, -0.22, 0.18)
    return jnp.clip(array, -reach, reach).astype(kind)


def setup_inputs(seed: int = 0, part: int = 0) -> dict:
    key_list = jax.random.split(jax.random.key(seed), 7)
    part_splits = jax.random.split(jax.random.fold_in(key_list[6], part), 7)
    inputs = bell_draw(part_splits[0], (TOKENS, D), 1.0, 6.0, ((0, 16),))
    out_grads = bell_draw(part_splits[1], (TOKENS, D), 1.0, 6.0, ((0, 16),))
    gates = jnp.clip(jnp.exp(math.log(0.8) - 2.7725887 * jax.random.uniform(part_splits[2], (TOKENS, TOPK), jnp.float32) ** block_scale(part_splits[2], (TOKENS, TOPK), ((0, 16),), -0.2, 0.2)), 0.05, 0.8)
    expert_ids_keys = jax.random.split(jax.random.fold_in(part_splits[3], 1), TOKENS // TOK_DEV)
    expert_ids_turns = jax.random.permutation(jax.random.fold_in(part_splits[3], 3), TOKENS // TOK_DEV)
    expert_ids = jax.vmap(lambda own, number: assign_block(jax.random.fold_in(part_splits[3], 2), own, number, TOK_DEV, EXPERTS, TOPK, CAP, 2))(expert_ids_keys, expert_ids_turns).reshape((TOKENS, TOPK))
    offsets = draw_offsets(jax.random.fold_in(jax.random.fold_in(key_list[6], part), 71), part)
    projections = bell_draw(key_list[5], (D, 2 * RANK), D ** -0.5, 0.0625)
    return dict(inputs=inputs, out_grads=out_grads, gates=gates, expert_ids=expert_ids, offsets=offsets, projections=projections)


def reference(inputs, out_grads, gates, expert_ids, offsets, projections):
    rank = projections.shape[1] // 2
    a_rows = jnp.dot(inputs, projections[:, :rank], preferred_element_type=jnp.float32).astype(jnp.bfloat16)
    b_full = jnp.dot(out_grads, projections[:, rank:], preferred_element_type=jnp.float32)
    position = jnp.arange(TOKENS, dtype=jnp.int32)
    doc = lax.optimization_barrier(jnp.sum((position[:, None] >= offsets[None, 1:DOCS]).astype(jnp.int32), axis=1)).astype(jnp.int32)
    lengths = (offsets[1:] - offsets[:-1]).astype(jnp.float32)
    doc_hot = doc[:, None] == jnp.arange(DOCS, dtype=jnp.int32)[None, :]
    length_tok = lax.optimization_barrier(jnp.sum(jnp.where(doc_hot, lengths[None, :], jnp.zeros((), jnp.float32)), axis=1))
    inverse = lax.rsqrt(length_tok)
    shared_rows = (b_full * inverse[:, None]).astype(jnp.bfloat16)
    route_scale = (EXPERTS / TOPK) ** 0.5
    routed = (gates[:, :, None] * (route_scale * inverse)[:, None, None] * b_full[:, None, :]).astype(jnp.bfloat16)
    masked = jnp.where(doc_hot[:, :, None], shared_rows[:, None, :], jnp.zeros((), jnp.bfloat16)).reshape(TOKENS, DOCS * rank)
    shared = jnp.dot(masked.T, a_rows, preferred_element_type=jnp.float32).reshape(DOCS, rank * rank)
    segments = (expert_ids * DOCS + doc[:, None]).astype(jnp.int32)

    def add_block(index, total):
        begin = (index * TOK_DEV).astype(jnp.int32)
        routed_blk = lax.dynamic_slice_in_dim(routed, begin, TOK_DEV, 0).astype(jnp.float32)
        a_blk = lax.dynamic_slice_in_dim(a_rows, begin, TOK_DEV, 0).astype(jnp.float32)
        seg_blk = lax.dynamic_slice_in_dim(segments, begin, TOK_DEV, 0)
        outer = routed_blk[:, :, :, None] * a_blk[:, None, None, :]
        return total + jax.ops.segment_sum(outer.reshape(TOK_DEV * TOPK, rank * rank), seg_blk.reshape(-1), num_segments=EXPERTS * DOCS)
    total = lax.fori_loop(0, TOKENS // TOK_DEV, add_block, jnp.zeros((EXPERTS * DOCS, rank * rank), jnp.float32))
    return (shared, total.reshape(EXPERTS, DOCS, rank * rank))
```

```python
import functools

import jax
import jax.numpy as jnp
from jax import lax
from jax.experimental import pallas as pl
from jax.experimental.pallas import tpu as pltpu
from jax.sharding import PartitionSpec as P

EXPERTS = 256
TOPK = 8
DOCS = 8
CHUNK = 1024
VMEM_LIMIT = 48 * 1024 * 1024


def doc_of(offsets_ref, start):
    doc = jnp.int32(0)
    for i in range(1, DOCS):
        doc = doc + (start >= offsets_ref[i]).astype(jnp.int32)
    return doc


def project_kernel(
    where_ref, offsets_ref, gates_ref, ids_ref, x_hbm, g_hbm, p_hbm, out_ref,
    x_buf, g_buf, p_buf, rows_buf, x_sem, g_sem, p_sem,
):
    tok, depth = x_hbm.shape
    rank = p_hbm.shape[1] // 2
    half = rank // 2
    chunks = depth // CHUNK

    def copies(i):
        cols = pl.ds(i * CHUNK, CHUNK)
        return (
            pltpu.make_async_copy(p_hbm.at[cols, :], p_buf.at[cols, :], p_sem.at[i]),
            pltpu.make_async_copy(x_hbm.at[:, cols], x_buf.at[:, cols], x_sem.at[i]),
            pltpu.make_async_copy(g_hbm.at[:, cols], g_buf.at[:, cols], g_sem.at[i]),
        )

    for i in range(chunks):
        for copy in copies(i):
            copy.start()
    a = jnp.zeros((tok, rank), jnp.float32)
    b = jnp.zeros((tok, rank), jnp.float32)
    for i in range(chunks):
        for copy in copies(i):
            copy.wait()
        cols = pl.ds(i * CHUNK, CHUNK)
        a = a + jnp.dot(
            x_buf[:, cols], p_buf[cols, :rank], preferred_element_type=jnp.float32
        )
        b = b + jnp.dot(
            g_buf[:, cols], p_buf[cols, rank:], preferred_element_type=jnp.float32
        )
    start = where_ref[0]
    first = doc_of(offsets_ref, start)
    second = jnp.minimum(first + 1, DOCS - 1)
    position = start + lax.broadcasted_iota(jnp.int32, (1, tok), 1)
    in_first = position < offsets_ref[first + 1]
    length = jnp.where(
        in_first,
        offsets_ref[first + 1] - offsets_ref[first],
        offsets_ref[second + 1] - offsets_ref[second],
    ).astype(jnp.float32)
    scale = lax.rsqrt(length)
    both = jnp.concatenate([a, b], axis=1).T
    out_ref[:rank, :] = both[:rank, :].astype(jnp.bfloat16)
    scaled = both[rank:, :] * scale
    for j in range(tok // 128):
        lanes = slice(j * 128, (j + 1) * 128)
        rows_buf[j, :, :] = scaled[:, lanes]
        for odd in range(2):
            picked = rows_buf[j, pl.ds(odd, half, stride=2), :]
            place = rank + odd * half
            out_ref[place : place + half, lanes] = picked.astype(jnp.bfloat16)
    gates = gates_ref[...]
    high = gates.astype(jnp.bfloat16).astype(jnp.float32)
    ids = ids_ref[...].astype(jnp.float32)
    out_ref[2 * rank : 2 * rank + 16, :] = jnp.concatenate([ids, high], axis=0).astype(jnp.bfloat16)
    out_ref[2 * rank + 16 :, :] = jnp.concatenate(
        [gates - high, jnp.zeros_like(gates)], axis=0
    ).astype(jnp.bfloat16)


def sum_kernel(
    experts, where_ref, offsets_ref, own_ref, other_ref, routed_ref, shared_ref, acc, tiles
):
    height, tok = 160, own_ref.shape[1]
    slots = own_ref.shape[0] // height
    rank = 64
    half = rank // 2
    me = where_ref[0]
    route_scale = (EXPERTS / TOPK) ** 0.5
    acc[...] = jnp.zeros_like(acc)

    def block(ref, source, base):
        start = source * tok
        first = doc_of(offsets_ref, start)
        edge = offsets_ref[first + 1]
        position = start + lax.broadcasted_iota(jnp.int32, (1, tok), 1)
        in_first = (position < edge).astype(jnp.float32)
        a = ref[pl.ds(base, rank), :].astype(jnp.float32)
        b = ref[pl.ds(base + rank, rank), :].astype(jnp.float32)
        named = ref[pl.ds(base + 2 * rank, 16), :].astype(jnp.float32)
        low = ref[pl.ds(base + 2 * rank + 16, 16), :].astype(jnp.float32)
        ids, gates = named[:8, :], (named[8:, :] + low[:8, :]) * route_scale
        even, odd = b[:half, :], b[half:, :]
        left = []
        for e in range(experts):
            mine = (me * experts + e).astype(jnp.float32)
            w = jnp.sum(jnp.where(ids == mine, gates, 0.0), axis=0, keepdims=True)
            left.append(jnp.concatenate([w * even, w * odd], axis=1).astype(jnp.bfloat16))
        left.append(jnp.concatenate([even, odd], axis=1).astype(jnp.bfloat16))
        left = jnp.concatenate(left, axis=0)
        a_first = a * in_first
        a_second = a - a_first
        none = jnp.zeros_like(a)
        right = jnp.concatenate(
            [
                jnp.concatenate([a_first, none], axis=1),
                jnp.concatenate([none, a_first], axis=1),
                jnp.concatenate([a_second, none], axis=1),
                jnp.concatenate([none, a_second], axis=1),
            ],
            axis=0,
        ).astype(jnp.bfloat16)
        both = lax.dot_general(
            left, right, (((1,), (1,)), ((), ())), preferred_element_type=jnp.float32
        )
        acc[first, :, :] += both[:, : 2 * rank]

        @pl.when(edge < start + tok)
        def _():
            acc[first + 1, :, :] += both[:, 2 * rank :]

    def step(s, _):
        base = pl.multiple_of(s * height, height)
        block(own_ref, where_ref[1 + s], base)
        block(other_ref, where_ref[1 + slots + s], base)
        return 0

    lax.fori_loop(0, slots, step, 0)
    rows = acc.shape[1]
    for d in range(DOCS):
        tiles[pl.ds(d, rows, stride=DOCS), :] = acc[d, :, :]
    for e in range(experts):
        for r in range(half):
            row = (e * half + r) * DOCS
            routed_ref[e, :, r * 128 : (r + 1) * 128] = tiles[row : row + DOCS, :]
    wide = shared_ref.shape[1] // 128
    place = experts * half + where_ref[1 + 2 * slots]
    for j in range(wide):
        row = pl.multiple_of((place + j) * DOCS, DOCS)
        shared_ref[:, j * 128 : (j + 1) * 128] = tiles[pl.ds(row, DOCS), :]


def on_device(devices, inputs, out_grads, gates, expert_ids, offsets, projections):
    tok, _ = inputs.shape
    rank = projections.shape[1] // 2
    half = rank // 2
    experts = EXPERTS // devices
    me = lax.axis_index("ctx").astype(jnp.int32)
    height = 2 * rank + 32
    smem = pl.BlockSpec(memory_space=pltpu.SMEM)
    vmem = pl.BlockSpec(memory_space=pltpu.VMEM)
    hbm = pl.BlockSpec(memory_space=pl.ANY)
    chunks = inputs.shape[1] // CHUNK
    payload = pl.pallas_call(
        project_kernel,
        out_shape=jax.ShapeDtypeStruct((height, tok), jnp.bfloat16),
        in_specs=[smem, smem, vmem, vmem, hbm, hbm, hbm],
        out_specs=vmem,
        scratch_shapes=[
            pltpu.VMEM(inputs.shape, jnp.bfloat16),
            pltpu.VMEM(inputs.shape, jnp.bfloat16),
            pltpu.VMEM(projections.shape, jnp.bfloat16),
            pltpu.VMEM((tok // 128, rank, 128), jnp.float32),
            pltpu.SemaphoreType.DMA((chunks,)),
            pltpu.SemaphoreType.DMA((chunks,)),
            pltpu.SemaphoreType.DMA((chunks,)),
        ],
        compiler_params=pltpu.CompilerParams(vmem_limit_bytes=VMEM_LIMIT),
        name="project",
    )((me * tok).reshape(1), offsets, gates.T, expert_ids.T, inputs, out_grads, projections)

    far = [1 << k for k in range(devices.bit_length() - 2, 0, -1)]
    order = (far, far[:1] + far[-1:] + far[1:-1] if len(far) > 2 else far)
    held, mask = payload, jnp.zeros((1,), jnp.int32)
    odd = (me & 1) == 1
    for k in range(len(far)):
        pairs = [(i, i ^ order[i & 1][k]) for i in range(devices)]
        got = lax.ppermute(held, "ctx", pairs)
        held = jnp.concatenate([held, got], axis=0)
        step = jnp.where(odd, order[1][k], order[0][k]).astype(jnp.int32)
        mask = jnp.concatenate([mask, mask ^ step])
    other = lax.ppermute(held, "ctx", [(i, i ^ 1) for i in range(devices)])
    other_mask = jnp.zeros((1,), jnp.int32)
    for k in range(len(far)):
        step = jnp.where(odd, order[0][k], order[1][k]).astype(jnp.int32)
        other_mask = jnp.concatenate([other_mask, other_mask ^ step])
    columns = rank * rank // devices
    where = jnp.concatenate(
        [me.reshape(1), me ^ mask, me ^ other_mask ^ 1, (me * columns // 128).reshape(1)]
    )
    rows = (experts + 1) * half
    routed, shared = pl.pallas_call(
        functools.partial(sum_kernel, experts),
        out_shape=(
            jax.ShapeDtypeStruct((experts, DOCS, rank * rank), jnp.float32),
            jax.ShapeDtypeStruct((DOCS, max(columns, 128)), jnp.float32),
        ),
        in_specs=[smem, smem, vmem, vmem],
        out_specs=(vmem, vmem),
        scratch_shapes=[
            pltpu.VMEM((DOCS, rows, 2 * rank), jnp.float32),
            pltpu.VMEM((DOCS * rows, 2 * rank), jnp.float32),
        ],
        compiler_params=pltpu.CompilerParams(vmem_limit_bytes=VMEM_LIMIT),
        name="sums",
    )(where, offsets, held, other)
    if columns < 128:
        shared = lax.dynamic_slice_in_dim(shared, me * columns % 128, columns, 1)
    return shared, routed


def solution(mesh):
    placed = (
        P(("groups", "ctx"), None),
        P(("groups", "ctx"), None),
        P(("groups", "ctx"), None),
        P(("groups", "ctx"), None),
        P("groups"),
        P(),
    )
    return jax.shard_map(
        functools.partial(on_device, mesh.shape["ctx"]),
        mesh=mesh,
        in_specs=placed,
        out_specs=(P("groups", "ctx"), P("ctx", "groups", None)),
        check_vma=False,
    )
```

```python
import functools

import jax
import jax.numpy as jnp
from jax import lax
from jax.experimental import pallas as pl
from jax.experimental.pallas import tpu as pltpu
from jax.sharding import PartitionSpec as P

EXPERTS = 256
TOPK = 8
DOCS = 8
CHUNK = 3584
VMEM_LIMIT = 32 * 1024 * 1024


def doc_of(offsets_ref, start):
    doc = jnp.int32(0)
    for i in range(1, DOCS):
        doc = doc + (start >= offsets_ref[i]).astype(jnp.int32)
    return doc


def project_kernel(
    gates_hbm, ids_hbm, offsets_hbm, x_hbm, g_hbm, p_hbm, out_ref,
    gates_ref, ids_ref, offsets_ref, x_buf, g_buf, p_buf, rows_buf, x_sem, g_sem, p_sem, small_sem,
):
    tok, depth = x_hbm.shape
    rank = p_hbm.shape[1] // 2
    half = rank // 2
    chunks = depth // CHUNK
    small = (
        pltpu.make_async_copy(offsets_hbm, offsets_ref, small_sem.at[0]),
        pltpu.make_async_copy(gates_hbm, gates_ref, small_sem.at[1]),
        pltpu.make_async_copy(ids_hbm, ids_ref, small_sem.at[2]),
    )

    def copies(i):
        cols = pl.ds(i * CHUNK, CHUNK)
        return (
            pltpu.make_async_copy(p_hbm.at[cols, :], p_buf.at[cols, :], p_sem.at[i]),
            pltpu.make_async_copy(x_hbm.at[:, cols], x_buf.at[:, cols], x_sem.at[i]),
            pltpu.make_async_copy(g_hbm.at[:, cols], g_buf.at[:, cols], g_sem.at[i]),
        )

    for copy in copies(0) + small:
        copy.start()
    for i in range(1, chunks):
        for copy in copies(i):
            copy.start()
    for copy in small:
        copy.wait()
    gates = gates_ref[...]
    high = gates.astype(jnp.bfloat16).astype(jnp.float32)
    ids = ids_ref[...].astype(jnp.float32)
    out_ref[2 * rank : 2 * rank + 16, :] = jnp.concatenate([ids, high], axis=0).astype(jnp.bfloat16)
    out_ref[2 * rank + 16 :, :] = jnp.concatenate(
        [gates - high, jnp.zeros_like(gates)], axis=0
    ).astype(jnp.bfloat16)
    start = lax.axis_index("ctx").astype(jnp.int32) * tok
    first = doc_of(offsets_ref, start)
    second = jnp.minimum(first + 1, DOCS - 1)
    position = start + lax.broadcasted_iota(jnp.int32, (1, tok), 1)
    length = jnp.where(
        position < offsets_ref[first + 1],
        offsets_ref[first + 1] - offsets_ref[first],
        offsets_ref[second + 1] - offsets_ref[second],
    ).astype(jnp.float32)
    scale = lax.rsqrt(length)
    a = jnp.zeros((tok, rank), jnp.float32)
    b = jnp.zeros((tok, rank), jnp.float32)
    for i in range(chunks):
        for copy in copies(i)[:2]:
            copy.wait()
        cols = pl.ds(i * CHUNK, CHUNK)
        p = p_buf[cols, :]
        a = a + jnp.dot(x_buf[:, cols], p, preferred_element_type=jnp.float32)[:, :rank]
        copies(i)[2].wait()
        b = b + jnp.dot(g_buf[:, cols], p, preferred_element_type=jnp.float32)[:, rank:]
    both = jnp.concatenate([a, b], axis=1).T
    out_ref[:rank, :] = both[:rank, :].astype(jnp.bfloat16)
    scaled = both[rank:, :] * scale
    for j in range(tok // 128):
        lanes = slice(j * 128, (j + 1) * 128)
        rows_buf[j, :, :] = scaled[:, lanes]
        for odd in range(2):
            picked = rows_buf[j, pl.ds(odd, half, stride=2), :]
            place = rank + odd * half
            out_ref[place : place + half, lanes] = picked.astype(jnp.bfloat16)


def add_block(shape, offsets_ref, ref, base, source, me, acc):
    experts, rank = shape
    half = rank // 2
    tok = ref.shape[1]
    start = source * tok
    first = doc_of(offsets_ref, start)
    position = start + lax.broadcasted_iota(jnp.int32, (1, tok), 1)
    in_first = (position < offsets_ref[first + 1]).astype(jnp.float32)
    a = ref[pl.ds(base, rank), :].astype(jnp.float32)
    b = ref[pl.ds(base + rank, rank), :].astype(jnp.float32)
    named = ref[pl.ds(base + 2 * rank, 16), :].astype(jnp.float32)
    low = ref[pl.ds(base + 2 * rank + 16, 16), :].astype(jnp.float32)
    ids, gates = named[:8, :], (named[8:, :] + low[:8, :]) * (EXPERTS / TOPK) ** 0.5
    even, odd = b[:half, :], b[half:, :]
    left = []
    for e in range(experts):
        mine = (me * experts + e).astype(jnp.float32)
        w = jnp.sum(jnp.where(ids == mine, gates, 0.0), axis=0, keepdims=True)
        left.append(jnp.concatenate([w * even, w * odd], axis=1).astype(jnp.bfloat16))
    left.append(jnp.concatenate([even, odd], axis=1).astype(jnp.bfloat16))
    left = jnp.concatenate(left, axis=0)
    a_first = a * in_first
    a_second = (a - a_first).astype(jnp.bfloat16)
    a_first = a_first.astype(jnp.bfloat16)
    none = jnp.zeros_like(a_first)
    right = jnp.concatenate(
        [
            jnp.concatenate([a_first, none], axis=1),
            jnp.concatenate([none, a_first], axis=1),
            jnp.concatenate([a_second, none], axis=1),
            jnp.concatenate([none, a_second], axis=1),
        ],
        axis=0,
    )
    both = lax.dot_general(
        left, right, (((1,), (1,)), ((), ())), preferred_element_type=jnp.float32
    )
    acc[first, :, :] += both[:, : 2 * rank]
    acc[jnp.minimum(first + 1, DOCS - 1), :, :] += both[:, 2 * rank :]


def add_all(shape, order, blocks, height, offsets_ref, refs, acc):
    me = lax.axis_index("ctx").astype(jnp.int32)
    stages = len(order[0])

    def source(slot, tag, flip):
        origin = me ^ flip
        path = slot | tag
        for k in range(stages):
            hop = jnp.where((origin & 1) == 1, order[1][k], order[0][k])
            origin = origin ^ (((path >> k) & 1) * hop)
        return origin

    slots = refs[0].shape[0] // height
    if slots <= 4:
        for ref, (tag, flip) in zip(refs, blocks):
            for s in range(slots):
                add_block(shape, offsets_ref, ref, s * height, source(s, tag, flip), me, acc)
        return

    def step(s, _):
        base = pl.multiple_of(s * height, height)
        for ref, (tag, flip) in zip(refs, blocks):
            add_block(shape, offsets_ref, ref, base, source(s, tag, flip), me, acc)
        return 0

    lax.fori_loop(0, slots, step, 0)


def first_kernel(shape, order, blocks, height, offsets_ref, *refs):
    acc = refs[-1]
    acc[...] = jnp.zeros_like(acc)
    add_all(shape, order, blocks, height, offsets_ref, refs[:-1], acc)


def next_kernel(shape, order, blocks, height, offsets_ref, held, *refs):
    add_all(shape, order, blocks, height, offsets_ref, refs[:-1], refs[-1])


def last_kernel(shape, order, blocks, height, offsets_ref, held, *refs):
    experts, rank = shape
    half = rank // 2
    refs, (routed_hbm, shared_ref, acc, sem) = refs[:-4], refs[-4:]
    add_all(shape, order, blocks, height, offsets_ref, refs, acc)
    copies = [
        pltpu.make_async_copy(
            acc.at[d, pl.ds(0, experts * half), :], routed_hbm.at[:, d, :], sem.at[d]
        )
        for d in range(DOCS)
    ]
    for copy in copies:
        copy.start()
    me = lax.axis_index("ctx").astype(jnp.int32)
    columns = rank * rank * experts // EXPERTS
    place = experts * half + me * columns // 128
    for j in range(shared_ref.shape[1] // 128):
        for d in range(DOCS):
            shared_ref[d : d + 1, j * 128 : (j + 1) * 128] = acc[d, pl.ds(place + j, 1), :]
    for copy in copies:
        copy.wait()


def on_device(devices, inputs, out_grads, gates, expert_ids, offsets, projections):
    tok, _ = inputs.shape
    rank = projections.shape[1] // 2
    half = rank // 2
    experts = EXPERTS // devices
    height = 2 * rank + 32
    smem = pl.BlockSpec(memory_space=pltpu.SMEM)
    vmem = pl.BlockSpec(memory_space=pltpu.VMEM)
    hbm = pl.BlockSpec(memory_space=pltpu.HBM)
    chunks = inputs.shape[1] // CHUNK
    params = pltpu.CompilerParams(vmem_limit_bytes=VMEM_LIMIT)

    def in_place(x):
        return pltpu.with_memory_space_constraint(x, pltpu.HBM)

    payload = pl.pallas_call(
        project_kernel,
        out_shape=pltpu.VMEM((height, tok), jnp.bfloat16),
        in_specs=[hbm] * 6,
        out_specs=vmem,
        scratch_shapes=[
            pltpu.VMEM((TOPK, tok), jnp.float32),
            pltpu.VMEM((TOPK, tok), jnp.int32),
            pltpu.SMEM(offsets.shape, jnp.int32),
            pltpu.VMEM(inputs.shape, jnp.bfloat16),
            pltpu.VMEM(inputs.shape, jnp.bfloat16),
            pltpu.VMEM(projections.shape, jnp.bfloat16),
            pltpu.VMEM((tok // 128, rank, 128), jnp.float32),
            pltpu.SemaphoreType.DMA((chunks,)),
            pltpu.SemaphoreType.DMA((chunks,)),
            pltpu.SemaphoreType.DMA((chunks,)),
            pltpu.SemaphoreType.DMA((3,)),
        ],
        compiler_params=params,
        name="project",
    )(*(in_place(x) for x in (gates.T, expert_ids.T, offsets, inputs, out_grads, projections)))

    far = [1 << k for k in range(devices.bit_length() - 2, 0, -1)]
    order = (far, far[-1:] + far[:-1])
    last = len(far) - 1

    def swap(block, k):
        return lax.ppermute(block, "ctx", [(i, i ^ order[i & 1][k]) for i in range(devices)])

    def core(block):
        return lax.ppermute(block, "ctx", [(i, i ^ 1) for i in range(devices)])

    def after(block, acc):
        return lax.optimization_barrier((block, acc))

    shape = (experts, rank)
    rows = (experts + 1) * half
    sums = pltpu.VMEM((DOCS, rows, 2 * rank), jnp.float32)

    def add(name, blocks, acc=None):
        held = [] if acc is None else [acc]
        kernel = first_kernel if acc is None else next_kernel
        return pl.pallas_call(
            functools.partial(kernel, shape, order, [b[1:] for b in blocks], height),
            out_shape=sums,
            in_specs=[smem] + [vmem] * (len(blocks) + len(held)),
            out_specs=vmem,
            input_output_aliases={1: 0} if held else {},
            compiler_params=params,
            name=name,
        )(offsets, *held, *(b[0] for b in blocks))

    near = payload
    for k in range(last - 1):
        near = jnp.concatenate([near, swap(near, k)], axis=0)
    bits = (1 << (last - 1), 1 << last)
    both = bits[0] | bits[1]
    one = swap(near, last - 1)
    two = swap(near, last)
    near_core = core(near)
    acc = add("sums_near", [(near, 0, 0), (near_core, 0, 1)])
    one, acc = after(one, acc)
    three = swap(one, last)
    one_core, two_core = core(one), core(two)
    blocks = [(one, bits[0], 0), (one_core, bits[0], 1), (two, bits[1], 0), (two_core, bits[1], 1)]
    acc = add("sums_next", blocks, acc)
    three, acc = after(three, acc)
    three_core = core(three)
    acc = add("sums_three", [(three, both, 0)], acc)
    three_core, acc = after(three_core, acc)
    blocks = [(three_core, both, 1)]
    columns = rank * rank // devices
    routed, shared, _ = pl.pallas_call(
        functools.partial(last_kernel, shape, order, [b[1:] for b in blocks], height),
        out_shape=(
            jax.ShapeDtypeStruct((experts * half, DOCS, 2 * rank), jnp.float32),
            jax.ShapeDtypeStruct((DOCS, max(columns, 128)), jnp.float32),
            sums,
        ),
        in_specs=[smem] + [vmem] * (len(blocks) + 1),
        out_specs=(hbm, vmem, vmem),
        scratch_shapes=[pltpu.SemaphoreType.DMA((DOCS,))],
        input_output_aliases={1: 2},
        compiler_params=params,
        name="sums_last",
    )(offsets, acc, *(b[0] for b in blocks))
    routed = routed.reshape(experts, half, DOCS, 2 * rank).transpose(0, 2, 1, 3)
    routed = routed.reshape(experts, DOCS, rank * rank)
    if columns < 128:
        me = lax.axis_index("ctx")
        shared = lax.dynamic_slice_in_dim(shared, me * columns % 128, columns, 1)
    return shared, routed


def solution(mesh):
    placed = (
        P(("groups", "ctx"), None),
        P(("groups", "ctx"), None),
        P(("groups", "ctx"), None),
        P(("groups", "ctx"), None),
        P("groups"),
        P(),
    )
    return jax.shard_map(
        functools.partial(on_device, mesh.shape["ctx"]),
        mesh=mesh,
        in_specs=placed,
        out_specs=(P("groups", "ctx"), P("ctx", "groups", None)),
        check_vma=False,
    )
```

```python
import functools

import jax
import jax.numpy as jnp
from jax import lax
from jax.experimental import pallas as pl
from jax.experimental.pallas import tpu as pltpu
from jax.sharding import PartitionSpec as P

EXPERTS = 256
TOPK = 8
DOCS = 8
CHUNK = 3584
FLUSH = 2
VMEM_LIMIT = 32 * 1024 * 1024


def doc_of(offsets_ref, start):
    doc = jnp.int32(0)
    for i in range(1, DOCS):
        doc = doc + (start >= offsets_ref[i]).astype(jnp.int32)
    return doc


def project_kernel(
    gates_hbm, ids_hbm, offsets_hbm, x_hbm, g_hbm, p_hbm, out_ref, offsets_ref,
    gates_ref, ids_ref, x_buf, g_buf, p_buf, rows_buf, x_sem, g_sem, p_sem, small_sem,
):
    tok, depth = x_hbm.shape
    rank = p_hbm.shape[1] // 2
    half = rank // 2
    chunks = depth // CHUNK
    small = (
        pltpu.make_async_copy(offsets_hbm, offsets_ref, small_sem.at[0]),
        pltpu.make_async_copy(gates_hbm, gates_ref, small_sem.at[1]),
        pltpu.make_async_copy(ids_hbm, ids_ref, small_sem.at[2]),
    )

    def copies(i):
        cols = pl.ds(i * CHUNK, CHUNK)
        return (
            pltpu.make_async_copy(p_hbm.at[cols, :], p_buf.at[cols, :], p_sem.at[i]),
            pltpu.make_async_copy(x_hbm.at[:, cols], x_buf.at[:, cols], x_sem.at[i]),
            pltpu.make_async_copy(g_hbm.at[:, cols], g_buf.at[:, cols], g_sem.at[i]),
        )

    for copy in copies(0) + small:
        copy.start()
    for i in range(1, chunks):
        for copy in copies(i):
            copy.start()
    for copy in small:
        copy.wait()
    gates = gates_ref[...]
    high = gates.astype(jnp.bfloat16).astype(jnp.float32)
    ids = ids_ref[...].astype(jnp.float32)
    out_ref[2 * rank : 2 * rank + 16, :] = jnp.concatenate([ids, high], axis=0).astype(jnp.bfloat16)
    out_ref[2 * rank + 16 :, :] = jnp.concatenate(
        [gates - high, jnp.zeros_like(gates)], axis=0
    ).astype(jnp.bfloat16)
    start = lax.axis_index("ctx").astype(jnp.int32) * tok
    first = doc_of(offsets_ref, start)
    second = jnp.minimum(first + 1, DOCS - 1)
    position = start + lax.broadcasted_iota(jnp.int32, (1, tok), 1)
    length = jnp.where(
        position < offsets_ref[first + 1],
        offsets_ref[first + 1] - offsets_ref[first],
        offsets_ref[second + 1] - offsets_ref[second],
    ).astype(jnp.float32)
    scale = lax.rsqrt(length)
    a = jnp.zeros((tok, rank), jnp.float32)
    b = jnp.zeros((tok, rank), jnp.float32)
    for i in range(chunks):
        for copy in copies(i)[:2]:
            copy.wait()
        cols = pl.ds(i * CHUNK, CHUNK)
        p = p_buf[cols, :]
        a = a + jnp.dot(x_buf[:, cols], p, preferred_element_type=jnp.float32)[:, :rank]
        copies(i)[2].wait()
        b = b + jnp.dot(g_buf[:, cols], p, preferred_element_type=jnp.float32)[:, rank:]
    both = jnp.concatenate([a, b], axis=1).T
    out_ref[:rank, :] = both[:rank, :].astype(jnp.bfloat16)
    scaled = both[rank:, :] * scale
    for j in range(tok // 128):
        lanes = slice(j * 128, (j + 1) * 128)
        rows_buf[j, :, :] = scaled[:, lanes]
        for odd in range(2):
            picked = rows_buf[j, pl.ds(odd, half, stride=2), :]
            place = rank + odd * half
            out_ref[place : place + half, lanes] = picked.astype(jnp.bfloat16)


def prepare(shape, offsets_ref, ref, base, source):
    rank = shape[1]
    half = rank // 2
    tok = ref.shape[1]
    start = source * tok
    first = doc_of(offsets_ref, start)
    position = start + lax.broadcasted_iota(jnp.int32, (1, tok), 1)
    in_first = (position < offsets_ref[first + 1]).astype(jnp.float32)
    a = ref[pl.ds(base, rank), :].astype(jnp.float32)
    b = ref[pl.ds(base + rank, rank), :].astype(jnp.float32)
    named = ref[pl.ds(base + 2 * rank, 16), :].astype(jnp.float32)
    low = ref[pl.ds(base + 2 * rank + 16, 16), :].astype(jnp.float32)
    ids, gates = named[:8, :], (named[8:, :] + low[:8, :]) * (EXPERTS / TOPK) ** 0.5
    a_first = a * in_first
    a_second = (a - a_first).astype(jnp.bfloat16)
    a_first = a_first.astype(jnp.bfloat16)
    none = jnp.zeros_like(a_first)
    right = jnp.concatenate(
        [
            jnp.concatenate([a_first, none], axis=1),
            jnp.concatenate([none, a_first], axis=1),
            jnp.concatenate([a_second, none], axis=1),
            jnp.concatenate([none, a_second], axis=1),
        ],
        axis=0,
    )
    docs = first, jnp.minimum(first + 1, DOCS - 1)
    return docs, ids, gates, b[:half, :], b[half:, :], right


def add_block(shape, block, me, acc, again, begin=0, end=None):
    experts, rank = shape
    half = rank // 2
    (first, second), ids, gates, even, odd, right = block
    end = experts + 1 if end is None else end
    left = []
    for e in range(begin, end):
        if e == experts:
            left.append(jnp.concatenate([even, odd], axis=1).astype(jnp.bfloat16))
            continue
        mine = (me * experts + e).astype(jnp.float32)
        w = jnp.sum(jnp.where(ids == mine, gates, 0.0), axis=0, keepdims=True)
        left.append(jnp.concatenate([w * even, w * odd], axis=1).astype(jnp.bfloat16))
    left = jnp.concatenate(left, axis=0)
    both = lax.dot_general(
        left, right, (((1,), (1,)), ((), ())), preferred_element_type=jnp.float32
    )
    rows = pl.ds(begin * half, (end - begin) * half)
    acc[first, rows, :] += both[:, : 2 * rank]
    again[second, rows, :] += both[:, 2 * rank :]


def origin_of(order, me, slot, tag, flip):
    origin = me ^ flip
    path = slot | tag
    for k in range(len(order[0])):
        hop = jnp.where((origin & 1) == 1, order[1][k], order[0][k])
        origin = origin ^ (((path >> k) & 1) * hop)
    return origin


def add_all(shape, order, blocks, height, offsets_ref, refs, acc, again):
    me = lax.axis_index("ctx").astype(jnp.int32)
    slots = refs[0].shape[0] // height

    def add(ref, s, base, tag, flip):
        source = origin_of(order, me, s, tag, flip)
        add_block(shape, prepare(shape, offsets_ref, ref, base, source), me, acc, again)

    if slots <= 4:
        for ref, (tag, flip) in zip(refs, blocks):
            for s in range(slots):
                add(ref, s, s * height, tag, flip)
        return

    def step(s, _):
        for ref, (tag, flip) in zip(refs, blocks):
            add(ref, s, pl.multiple_of(s * height, height), tag, flip)
        return 0

    lax.fori_loop(0, slots, step, 0)


def first_kernel(shape, order, blocks, height, offsets_ref, *refs):
    refs, (acc, again) = refs[:-2], refs[-2:]
    acc[...] = jnp.zeros_like(acc)
    again[...] = jnp.zeros_like(again)
    add_all(shape, order, blocks, height, offsets_ref, refs, acc, again)


def next_kernel(shape, order, blocks, height, offsets_ref, acc_in, again_in, *refs):
    add_all(shape, order, blocks, height, offsets_ref, refs[:-2], *refs[-2:])


def fold_kernel(shape, order, blocks, height, offsets_ref, acc_in, again, *refs):
    refs, acc = refs[:-1], refs[-1]
    add_all(shape, order, blocks, height, offsets_ref, refs, acc, again)
    acc[...] += again[...]


def last_kernel(shape, order, blocks, height, offsets_ref, held, *refs):
    experts, rank = shape
    half = rank // 2
    refs, (routed_hbm, shared_hbm, acc, shared_buf, sem) = refs[:-5], refs[-5:]
    me = lax.axis_index("ctx").astype(jnp.int32)
    slots = refs[0].shape[0] // height
    if slots <= 4:
        ready = [
            prepare(shape, offsets_ref, ref, s * height, origin_of(order, me, s, tag, flip))
            for ref, (tag, flip) in zip(refs, blocks)
            for s in range(slots)
        ]
    else:
        ready = []
        add_all(shape, order, blocks, height, offsets_ref, refs, acc, acc)
    cuts = [experts * k // FLUSH for k in range(FLUSH + 1)]
    copies = []
    for k in range(FLUSH):
        for block in ready:
            add_block(shape, block, me, acc, acc, cuts[k], cuts[k + 1] + (k == FLUSH - 1))
        rows = pl.ds(cuts[k] * half, (cuts[k + 1] - cuts[k]) * half)
        for d in range(DOCS):
            copies.append(
                pltpu.make_async_copy(acc.at[d, rows, :], routed_hbm.at[rows, d, :], sem.at[k, d])
            )
            copies[-1].start()
    columns = rank * rank * experts // EXPERTS
    place = experts * half + me * columns // 128
    for j in range(shared_buf.shape[1] // 128):
        for d in range(DOCS):
            shared_buf[d : d + 1, j * 128 : (j + 1) * 128] = acc[d, pl.ds(place + j, 1), :]
    copies.append(pltpu.make_async_copy(shared_buf, shared_hbm, sem.at[FLUSH, 0]))
    copies[-1].start()
    for copy in copies:
        copy.wait()


def on_device(devices, inputs, out_grads, gates, expert_ids, offsets, projections):
    tok, _ = inputs.shape
    rank = projections.shape[1] // 2
    half = rank // 2
    experts = EXPERTS // devices
    height = 2 * rank + 32
    smem = pl.BlockSpec(memory_space=pltpu.SMEM)
    vmem = pl.BlockSpec(memory_space=pltpu.VMEM)
    hbm = pl.BlockSpec(memory_space=pltpu.HBM)
    chunks = inputs.shape[1] // CHUNK
    params = pltpu.CompilerParams(vmem_limit_bytes=VMEM_LIMIT)

    def in_place(x):
        return pltpu.with_memory_space_constraint(x, pltpu.HBM)

    payload, offsets = pl.pallas_call(
        project_kernel,
        out_shape=(
            pltpu.VMEM((height, tok), jnp.bfloat16),
            pltpu.SMEM(offsets.shape, jnp.int32),
        ),
        in_specs=[hbm] * 6,
        out_specs=(vmem, smem),
        scratch_shapes=[
            pltpu.VMEM((TOPK, tok), jnp.float32),
            pltpu.VMEM((TOPK, tok), jnp.int32),
            pltpu.VMEM(inputs.shape, jnp.bfloat16),
            pltpu.VMEM(inputs.shape, jnp.bfloat16),
            pltpu.VMEM(projections.shape, jnp.bfloat16),
            pltpu.VMEM((tok // 128, rank, 128), jnp.float32),
            pltpu.SemaphoreType.DMA((chunks,)),
            pltpu.SemaphoreType.DMA((chunks,)),
            pltpu.SemaphoreType.DMA((chunks,)),
            pltpu.SemaphoreType.DMA((3,)),
        ],
        compiler_params=params,
        name="project",
    )(*(in_place(x) for x in (gates.T, expert_ids.T, offsets, inputs, out_grads, projections)))

    far = [1 << k for k in range(devices.bit_length() - 2, 0, -1)]
    order = (far[:1] + far[-1:] + far[1:-1], far[1:-1] + far[:1] + far[-1:])
    last = len(far) - 1

    def swap(block, k):
        return lax.ppermute(block, "ctx", [(i, i ^ order[i & 1][k]) for i in range(devices)])

    def core(block):
        return lax.ppermute(block, "ctx", [(i, i ^ 1) for i in range(devices)])

    def after(block, acc):
        return lax.optimization_barrier((block, acc))

    shape = (experts, rank)
    rows = (experts + 1) * half
    sums = pltpu.VMEM((DOCS, rows, 2 * rank), jnp.float32)

    def add(name, blocks, acc=(), fold=False):
        kernel = fold_kernel if fold else next_kernel if acc else first_kernel
        return pl.pallas_call(
            functools.partial(kernel, shape, order, [b[1:] for b in blocks], height),
            out_shape=sums if fold else (sums, sums),
            in_specs=[smem] + [vmem] * (len(blocks) + len(acc)),
            out_specs=vmem if fold else (vmem, vmem),
            input_output_aliases={1: 0} if fold else {1: 0, 2: 1} if acc else {},
            compiler_params=params,
            name=name,
        )(offsets, *acc, *(b[0] for b in blocks))

    near = payload
    acc = add("sums_own", [(payload, 0, 0)])
    for k in range(last - 1):
        got = swap(near, k)
        got, acc = after(got, acc)
        near = jnp.concatenate([near, got], axis=0)
        if k < last - 2:
            acc = add("sums_got", [(got, 1 << k, 0)], acc)
    bits = (1 << (last - 1), 1 << last)
    both = bits[0] | bits[1]
    one = swap(near, last - 1)
    acc = add("sums_got", [(got, 1 << (last - 2), 0)], acc)
    near, acc = after(near, acc)
    two = swap(near, last)
    near_core = core(near)
    one, acc = after(one, acc)
    three = swap(one, last)
    acc = add("sums_next", [(one, bits[0], 0), (two, bits[1], 0), (near_core, 0, 1)], acc)
    one, two, acc = lax.optimization_barrier((one, two, acc))
    one_core, two_core = core(one), core(two)
    three, acc = after(three, acc)
    three_core = core(three)
    blocks = [(three, both, 0), (one_core, bits[0], 1), (two_core, bits[1], 1)]
    acc = add("sums_three", blocks, acc, fold=True)
    three_core, acc = after(three_core, acc)
    blocks = [(three_core, both, 1)]
    columns = rank * rank // devices
    routed, shared, _ = pl.pallas_call(
        functools.partial(last_kernel, shape, order, [b[1:] for b in blocks], height),
        out_shape=(
            jax.ShapeDtypeStruct((experts * half, DOCS, 2 * rank), jnp.float32),
            jax.ShapeDtypeStruct((DOCS, max(columns, 128)), jnp.float32),
            sums,
        ),
        in_specs=[smem] + [vmem] * (len(blocks) + 1),
        out_specs=(hbm, hbm, vmem),
        scratch_shapes=[
            pltpu.VMEM((DOCS, max(columns, 128)), jnp.float32),
            pltpu.SemaphoreType.DMA((FLUSH + 1, DOCS)),
        ],
        input_output_aliases={1: 2},
        compiler_params=params,
        name="sums_last",
    )(offsets, acc, *(b[0] for b in blocks))
    routed = routed.reshape(experts, half, DOCS, 2 * rank).transpose(0, 2, 1, 3)
    routed = routed.reshape(experts, DOCS, rank * rank)
    if columns < 128:
        me = lax.axis_index("ctx")
        shared = lax.dynamic_slice_in_dim(shared, me * columns % 128, columns, 1)
    return shared, routed


def solution(mesh):
    placed = (
        P(("groups", "ctx"), None),
        P(("groups", "ctx"), None),
        P(("groups", "ctx"), None),
        P(("groups", "ctx"), None),
        P("groups"),
        P(),
    )
    return jax.shard_map(
        functools.partial(on_device, mesh.shape["ctx"]),
        mesh=mesh,
        in_specs=placed,
        out_specs=(P("groups", "ctx"), P("ctx", "groups", None)),
        check_vma=False,
    )
```

```python
import functools

import jax
import jax.numpy as jnp
from jax import lax
from jax.experimental import pallas as pl
from jax.experimental.pallas import tpu as pltpu
from jax.sharding import PartitionSpec as P

EXPERTS = 256
TOPK = 8
DOCS = 8
CHUNK = 3584
VMEM_LIMIT = 32 * 1024 * 1024


def doc_of(offsets_ref, start):
    doc = jnp.int32(0)
    for i in range(1, DOCS):
        doc = doc + (start >= offsets_ref[i]).astype(jnp.int32)
    return doc


def project_kernel(
    gates_hbm, ids_hbm, offsets_hbm, x_hbm, g_hbm, p_hbm, out_ref, offsets_ref,
    gates_ref, ids_ref, x_buf, g_buf, p_buf, rows_buf, x_sem, g_sem, p_sem, small_sem,
):
    tok, depth = x_hbm.shape
    rank = p_hbm.shape[1] // 2
    half = rank // 2
    chunks = depth // CHUNK
    small = (
        pltpu.make_async_copy(offsets_hbm, offsets_ref, small_sem.at[0]),
        pltpu.make_async_copy(gates_hbm, gates_ref, small_sem.at[1]),
        pltpu.make_async_copy(ids_hbm, ids_ref, small_sem.at[2]),
    )

    def copies(i):
        cols = pl.ds(i * CHUNK, CHUNK)
        return (
            pltpu.make_async_copy(p_hbm.at[cols, :], p_buf.at[cols, :], p_sem.at[i]),
            pltpu.make_async_copy(x_hbm.at[:, cols], x_buf.at[:, cols], x_sem.at[i]),
            pltpu.make_async_copy(g_hbm.at[:, cols], g_buf.at[:, cols], g_sem.at[i]),
        )

    for copy in copies(0) + small:
        copy.start()
    for i in range(1, chunks):
        for copy in copies(i):
            copy.start()
    for copy in small:
        copy.wait()
    gates = gates_ref[...]
    high = gates.astype(jnp.bfloat16).astype(jnp.float32)
    ids = ids_ref[...].astype(jnp.float32)
    base = 2 * rank // 16 * tok
    out_ref[:, base : base + tok] = jnp.concatenate([ids, high], axis=0).astype(jnp.bfloat16)
    low = gates - high
    out_ref[:, base + tok :] = jnp.concatenate(
        [low[:, : tok // 2], low[:, tok // 2 :]], axis=0
    ).astype(jnp.bfloat16)
    start = lax.axis_index("ctx").astype(jnp.int32) * tok
    first = doc_of(offsets_ref, start)
    second = jnp.minimum(first + 1, DOCS - 1)
    position = start + lax.broadcasted_iota(jnp.int32, (1, tok), 1)
    length = jnp.where(
        position < offsets_ref[first + 1],
        offsets_ref[first + 1] - offsets_ref[first],
        offsets_ref[second + 1] - offsets_ref[second],
    ).astype(jnp.float32)
    scale = lax.rsqrt(length)
    a = jnp.zeros((tok, rank), jnp.float32)
    b = jnp.zeros((tok, rank), jnp.float32)
    for i in range(chunks):
        for copy in copies(i)[:2]:
            copy.wait()
        cols = pl.ds(i * CHUNK, CHUNK)
        p = p_buf[cols, :]
        a = a + jnp.dot(x_buf[:, cols], p, preferred_element_type=jnp.float32)[:, :rank]
        copies(i)[2].wait()
        b = b + jnp.dot(g_buf[:, cols], p, preferred_element_type=jnp.float32)[:, rank:]
    both = jnp.concatenate([a, b], axis=1).T
    for k in range(rank // 16):
        rows = both[k * 16 : (k + 1) * 16, :]
        out_ref[:, k * tok : (k + 1) * tok] = rows.astype(jnp.bfloat16)
    scaled = both[rank:, :] * scale
    for j in range(tok // 128):
        lanes = slice(j * 128, (j + 1) * 128)
        rows_buf[j, :, :] = scaled[:, lanes]
        for odd in range(2):
            picked = rows_buf[j, pl.ds(odd, half, stride=2), :].astype(jnp.bfloat16)
            for k in range(half // 16):
                place = (rank + odd * half + k * 16) // 16 * tok + j * 128
                out_ref[:, place : place + 128] = picked[k * 16 : (k + 1) * 16, :]


def prepare(shape, offsets_ref, ref, base, source):
    rank = shape[1]
    half = rank // 2
    tok = 2 * ref.shape[1] // (4 * rank // 16 + 3)

    def rows(begin, count):
        parts = [
            ref[pl.ds(base, 16), k * tok : (k + 1) * tok]
            for k in range(begin // 16, (begin + count) // 16)
        ]
        return jnp.concatenate(parts, axis=0).astype(jnp.float32)

    start = source * tok
    first = doc_of(offsets_ref, start)
    position = start + lax.broadcasted_iota(jnp.int32, (1, tok), 1)
    in_first = (position < offsets_ref[first + 1]).astype(jnp.float32)
    a, b, named = rows(0, rank), rows(rank, rank), rows(2 * rank, 16)
    low = ref[pl.ds(base, 16), (2 * rank // 16 + 1) * tok :].astype(jnp.float32)
    low = jnp.concatenate([low[:8, :], low[8:, :]], axis=1)
    ids, gates = named[:8, :], (named[8:, :] + low) * (EXPERTS / TOPK) ** 0.5
    a_first = a * in_first
    a_second = (a - a_first).astype(jnp.bfloat16)
    a_first = a_first.astype(jnp.bfloat16)
    none = jnp.zeros_like(a_first)
    right = jnp.concatenate(
        [
            jnp.concatenate([a_first, none], axis=1),
            jnp.concatenate([none, a_first], axis=1),
            jnp.concatenate([a_second, none], axis=1),
            jnp.concatenate([none, a_second], axis=1),
        ],
        axis=0,
    )
    docs = first, jnp.minimum(first + 1, DOCS - 1)
    return docs, ids, gates, b[:half, :], b[half:, :], right


def add_block(shape, block, me, acc, again, begin=0, end=None):
    experts, rank = shape
    half = rank // 2
    (first, second), ids, gates, even, odd, right = block
    end = experts + 1 if end is None else end
    left = []
    for e in range(begin, end):
        if e == experts:
            left.append(jnp.concatenate([even, odd], axis=1).astype(jnp.bfloat16))
            continue
        mine = (me * experts + e).astype(jnp.float32)
        w = jnp.sum(jnp.where(ids == mine, gates, 0.0), axis=0, keepdims=True)
        left.append(jnp.concatenate([w * even, w * odd], axis=1).astype(jnp.bfloat16))
    left = jnp.concatenate(left, axis=0)
    both = lax.dot_general(
        left, right, (((1,), (1,)), ((), ())), preferred_element_type=jnp.float32
    )
    rows = pl.ds(begin * half, (end - begin) * half)
    acc[first, rows, :] += both[:, : 2 * rank]
    again[second, rows, :] += both[:, 2 * rank :]


def origin_of(order, me, slot, tag, flip):
    origin = me ^ flip
    path = slot | tag
    for k in range(len(order[0])):
        hop = jnp.where((origin & 1) == 1, order[1][k], order[0][k])
        origin = origin ^ (((path >> k) & 1) * hop)
    return origin


def add_all(shape, order, blocks, height, offsets_ref, refs, acc, again):
    me = lax.axis_index("ctx").astype(jnp.int32)
    slots = refs[0].shape[0] // height

    def add(ref, s, base, tag, flip):
        source = origin_of(order, me, s, tag, flip)
        add_block(shape, prepare(shape, offsets_ref, ref, base, source), me, acc, again)

    if slots <= 4:
        for ref, (tag, flip) in zip(refs, blocks):
            for s in range(slots):
                add(ref, s, s * height, tag, flip)
        return

    def step(s, _):
        for ref, (tag, flip) in zip(refs, blocks):
            add(ref, s, pl.multiple_of(s * height, height), tag, flip)
        return 0

    lax.fori_loop(0, slots, step, 0)


def first_kernel(shape, order, blocks, height, offsets_ref, *refs):
    refs, (acc, again) = refs[:-2], refs[-2:]
    acc[...] = jnp.zeros_like(acc)
    again[...] = jnp.zeros_like(again)
    add_all(shape, order, blocks, height, offsets_ref, refs, acc, again)


def next_kernel(shape, order, blocks, height, offsets_ref, acc_in, again_in, *refs):
    add_all(shape, order, blocks, height, offsets_ref, refs[:-2], *refs[-2:])


def fold_kernel(shape, order, blocks, height, offsets_ref, acc_in, again, *refs):
    refs, acc = refs[:-1], refs[-1]
    add_all(shape, order, blocks, height, offsets_ref, refs, acc, again)
    acc[...] += again[...]


def last_kernel(shape, order, blocks, height, offsets_ref, held, *refs):
    experts, rank = shape
    half = rank // 2
    refs, (routed_hbm, shared_hbm, acc, shared_buf, sem) = refs[:-5], refs[-5:]
    me = lax.axis_index("ctx").astype(jnp.int32)
    slots = refs[0].shape[0] // height
    if slots <= 4:
        ready = [
            prepare(shape, offsets_ref, ref, s * height, origin_of(order, me, s, tag, flip))
            for ref, (tag, flip) in zip(refs, blocks)
            for s in range(slots)
        ]
    else:
        ready = []
        add_all(shape, order, blocks, height, offsets_ref, refs, acc, acc)
    rows = pl.ds(0, experts * half)
    copies = [
        pltpu.make_async_copy(acc.at[d, rows, :], routed_hbm.at[rows, d, :], sem.at[d])
        for d in range(DOCS)
    ]
    touched = [
        functools.reduce(jnp.logical_or, [doc == d for block in ready for doc in block[0]])
        if ready
        else True
        for d in range(DOCS)
    ]
    if ready:
        for copy, later in zip(copies, touched):
            pl.when(jnp.logical_not(later))(copy.start)
    for block in ready:
        add_block(shape, block, me, acc, acc)
    for copy, later in zip(copies, touched):
        if ready:
            pl.when(later)(copy.start)
        else:
            copy.start()
    columns = rank * rank * experts // EXPERTS
    place = experts * half + me * columns // 128
    for j in range(shared_buf.shape[1] // 128):
        for d in range(DOCS):
            shared_buf[d : d + 1, j * 128 : (j + 1) * 128] = acc[d, pl.ds(place + j, 1), :]
    copies.append(pltpu.make_async_copy(shared_buf, shared_hbm, sem.at[DOCS]))
    copies[-1].start()
    for copy in copies:
        copy.wait()


def on_device(devices, inputs, out_grads, gates, expert_ids, offsets, projections):
    tok, _ = inputs.shape
    rank = projections.shape[1] // 2
    half = rank // 2
    experts = EXPERTS // devices
    height, width = 16, tok * (2 * rank // 16) + tok + tok // 2
    smem = pl.BlockSpec(memory_space=pltpu.SMEM)
    vmem = pl.BlockSpec(memory_space=pltpu.VMEM)
    hbm = pl.BlockSpec(memory_space=pltpu.HBM)
    chunks = inputs.shape[1] // CHUNK
    params = pltpu.CompilerParams(vmem_limit_bytes=VMEM_LIMIT)

    def in_place(x):
        return pltpu.with_memory_space_constraint(x, pltpu.HBM)

    payload, offsets = pl.pallas_call(
        project_kernel,
        out_shape=(
            pltpu.VMEM((height, width), jnp.bfloat16),
            pltpu.SMEM(offsets.shape, jnp.int32),
        ),
        in_specs=[hbm] * 6,
        out_specs=(vmem, smem),
        scratch_shapes=[
            pltpu.VMEM((TOPK, tok), jnp.float32),
            pltpu.VMEM((TOPK, tok), jnp.int32),
            pltpu.VMEM(inputs.shape, jnp.bfloat16),
            pltpu.VMEM(inputs.shape, jnp.bfloat16),
            pltpu.VMEM(projections.shape, jnp.bfloat16),
            pltpu.VMEM((tok // 128, rank, 128), jnp.float32),
            pltpu.SemaphoreType.DMA((chunks,)),
            pltpu.SemaphoreType.DMA((chunks,)),
            pltpu.SemaphoreType.DMA((chunks,)),
            pltpu.SemaphoreType.DMA((3,)),
        ],
        compiler_params=params,
        name="project",
    )(*(in_place(x) for x in (gates.T, expert_ids.T, offsets, inputs, out_grads, projections)))

    far = [1 << k for k in range(devices.bit_length() - 2, 0, -1)]
    order = (far[:1] + far[-1:] + far[1:-1], far[1:-1] + far[:1] + far[-1:])
    last = len(far) - 1

    def swap(block, k):
        return lax.ppermute(block, "ctx", [(i, i ^ order[i & 1][k]) for i in range(devices)])

    def core(block):
        return lax.ppermute(block, "ctx", [(i, i ^ 1) for i in range(devices)])

    def after(block, acc):
        return lax.optimization_barrier((block, acc))

    shape = (experts, rank)
    rows = (experts + 1) * half
    sums = pltpu.VMEM((DOCS, rows, 2 * rank), jnp.float32)

    def add(name, blocks, acc=(), fold=False):
        kernel = fold_kernel if fold else next_kernel if acc else first_kernel
        return pl.pallas_call(
            functools.partial(kernel, shape, order, [b[1:] for b in blocks], height),
            out_shape=sums if fold else (sums, sums),
            in_specs=[smem] + [vmem] * (len(blocks) + len(acc)),
            out_specs=vmem if fold else (vmem, vmem),
            input_output_aliases={1: 0} if fold else {1: 0, 2: 1} if acc else {},
            compiler_params=params,
            name=name,
        )(offsets, *acc, *(b[0] for b in blocks))

    near = payload
    acc = add("sums_own", [(payload, 0, 0)])
    for k in range(last - 1):
        got = swap(near, k)
        got, acc = after(got, acc)
        near = jnp.concatenate([near, got], axis=0)
        if k < last - 2:
            acc = add("sums_got", [(got, 1 << k, 0)], acc)
    bits = (1 << (last - 1), 1 << last)
    both = bits[0] | bits[1]
    one = swap(near, last - 1)
    acc = add("sums_got", [(got, 1 << (last - 2), 0)], acc)
    near, acc = after(near, acc)
    two = swap(near, last)
    near_core = core(near)
    one, acc = after(one, acc)
    three = swap(one, last)
    one_core = core(one)
    blocks = [(one, bits[0], 0), (two, bits[1], 0), (near_core, 0, 1), (one_core, bits[0], 1)]
    acc = add("sums_next", blocks, acc)
    two, acc = after(two, acc)
    two_core = core(two)
    three, acc = after(three, acc)
    three_core = core(three)
    acc = add("sums_three", [(three, both, 0), (two_core, bits[1], 1)], acc, fold=True)
    three_core, acc = after(three_core, acc)
    blocks = [(three_core, both, 1)]
    columns = rank * rank // devices
    routed, shared, _ = pl.pallas_call(
        functools.partial(last_kernel, shape, order, [b[1:] for b in blocks], height),
        out_shape=(
            jax.ShapeDtypeStruct((experts * half, DOCS, 2 * rank), jnp.float32),
            jax.ShapeDtypeStruct((DOCS, max(columns, 128)), jnp.float32),
            sums,
        ),
        in_specs=[smem] + [vmem] * (len(blocks) + 1),
        out_specs=(hbm, hbm, vmem),
        scratch_shapes=[
            pltpu.VMEM((DOCS, max(columns, 128)), jnp.float32),
            pltpu.SemaphoreType.DMA((DOCS + 1,)),
        ],
        input_output_aliases={1: 2},
        compiler_params=params,
        name="sums_last",
    )(offsets, acc, *(b[0] for b in blocks))
    routed = routed.reshape(experts, half, DOCS, 2 * rank).transpose(0, 2, 1, 3)
    routed = routed.reshape(experts, DOCS, rank * rank)
    if columns < 128:
        me = lax.axis_index("ctx")
        shared = lax.dynamic_slice_in_dim(shared, me * columns % 128, columns, 1)
    return shared, routed


def solution(mesh):
    placed = (
        P(("groups", "ctx"), None),
        P(("groups", "ctx"), None),
        P(("groups", "ctx"), None),
        P(("groups", "ctx"), None),
        P("groups"),
        P(),
    )
    return jax.shard_map(
        functools.partial(on_device, mesh.shape["ctx"]),
        mesh=mesh,
        in_specs=placed,
        out_specs=(P("groups", "ctx"), P("ctx", "groups", None)),
        check_vma=False,
    )
```

```python
import functools

import jax
import jax.numpy as jnp
from jax import lax
from jax.experimental import pallas as pl
from jax.experimental.pallas import tpu as pltpu
from jax.sharding import PartitionSpec as P

EXPERTS = 256
TOPK = 8
DOCS = 8
CHUNK = 3584
VMEM_LIMIT = 32 * 1024 * 1024


def doc_of(offsets_ref, start):
    doc = jnp.int32(0)
    for i in range(1, DOCS):
        doc = doc + (start >= offsets_ref[i]).astype(jnp.int32)
    return doc


def project_kernel(
    gates_hbm, ids_hbm, offsets_hbm, x_hbm, g_hbm, p_hbm, out_ref, offsets_ref,
    gates_ref, ids_ref, x_buf, g_buf, p_buf, rows_buf, x_sem, g_sem, p_sem, small_sem,
):
    tok, depth = x_hbm.shape
    rank = p_hbm.shape[1] // 2
    half = rank // 2
    chunks = depth // CHUNK
    small = (
        pltpu.make_async_copy(offsets_hbm, offsets_ref, small_sem.at[0]),
        pltpu.make_async_copy(gates_hbm, gates_ref, small_sem.at[1]),
        pltpu.make_async_copy(ids_hbm, ids_ref, small_sem.at[2]),
    )

    def copies(i):
        cols = pl.ds(i * CHUNK, CHUNK)
        return (
            pltpu.make_async_copy(p_hbm.at[cols, :], p_buf.at[cols, :], p_sem.at[i]),
            pltpu.make_async_copy(x_hbm.at[:, cols], x_buf.at[:, cols], x_sem.at[i]),
            pltpu.make_async_copy(g_hbm.at[:, cols], g_buf.at[:, cols], g_sem.at[i]),
        )

    for copy in copies(0) + small:
        copy.start()
    for i in range(1, chunks):
        for copy in copies(i):
            copy.start()
    for copy in small:
        copy.wait()
    gates = gates_ref[...]
    high = gates.astype(jnp.bfloat16).astype(jnp.float32)
    ids = ids_ref[...].astype(jnp.float32)
    base = 2 * rank // 16 * tok
    out_ref[:, base : base + tok] = jnp.concatenate([ids, high], axis=0).astype(jnp.bfloat16)
    low = gates - high
    out_ref[:, base + tok :] = jnp.concatenate(
        [low[:, : tok // 2], low[:, tok // 2 :]], axis=0
    ).astype(jnp.bfloat16)
    start = lax.axis_index("ctx").astype(jnp.int32) * tok
    first = doc_of(offsets_ref, start)
    second = jnp.minimum(first + 1, DOCS - 1)
    position = start + lax.broadcasted_iota(jnp.int32, (1, tok), 1)
    length = jnp.where(
        position < offsets_ref[first + 1],
        offsets_ref[first + 1] - offsets_ref[first],
        offsets_ref[second + 1] - offsets_ref[second],
    ).astype(jnp.float32)
    scale = lax.rsqrt(length)
    a = jnp.zeros((tok, rank), jnp.float32)
    b = jnp.zeros((tok, rank), jnp.float32)
    for i in range(chunks):
        for copy in copies(i)[:2]:
            copy.wait()
        cols = pl.ds(i * CHUNK, CHUNK)
        p = p_buf[cols, :]
        a = a + jnp.dot(x_buf[:, cols], p, preferred_element_type=jnp.float32)[:, :rank]
        copies(i)[2].wait()
        b = b + jnp.dot(g_buf[:, cols], p, preferred_element_type=jnp.float32)[:, rank:]
    both = jnp.concatenate([a, b], axis=1).T
    for k in range(rank // 16):
        rows = both[k * 16 : (k + 1) * 16, :]
        out_ref[:, k * tok : (k + 1) * tok] = rows.astype(jnp.bfloat16)
    scaled = both[rank:, :] * scale
    for j in range(tok // 128):
        lanes = slice(j * 128, (j + 1) * 128)
        rows_buf[j, :, :] = scaled[:, lanes]
        for odd in range(2):
            picked = rows_buf[j, pl.ds(odd, half, stride=2), :].astype(jnp.bfloat16)
            for k in range(half // 16):
                place = (rank + odd * half + k * 16) // 16 * tok + j * 128
                out_ref[:, place : place + 128] = picked[k * 16 : (k + 1) * 16, :]


def prepare(shape, offsets_ref, ref, base, source):
    rank = shape[1]
    half = rank // 2
    tok = 2 * ref.shape[1] // (4 * rank // 16 + 3)

    def rows(begin, count):
        parts = [
            ref[pl.ds(base, 16), k * tok : (k + 1) * tok]
            for k in range(begin // 16, (begin + count) // 16)
        ]
        return jnp.concatenate(parts, axis=0).astype(jnp.float32)

    start = source * tok
    first = doc_of(offsets_ref, start)
    position = start + lax.broadcasted_iota(jnp.int32, (1, tok), 1)
    in_first = (position < offsets_ref[first + 1]).astype(jnp.float32)
    a, b, named = rows(0, rank), rows(rank, rank), rows(2 * rank, 16)
    low = ref[pl.ds(base, 16), (2 * rank // 16 + 1) * tok :].astype(jnp.float32)
    low = jnp.concatenate([low[:8, :], low[8:, :]], axis=1)
    ids, gates = named[:8, :], (named[8:, :] + low) * (EXPERTS / TOPK) ** 0.5
    a_first = a * in_first
    a_second = (a - a_first).astype(jnp.bfloat16)
    a_first = a_first.astype(jnp.bfloat16)
    none = jnp.zeros_like(a_first)
    right = jnp.concatenate(
        [
            jnp.concatenate([a_first, none], axis=1),
            jnp.concatenate([none, a_first], axis=1),
            jnp.concatenate([a_second, none], axis=1),
            jnp.concatenate([none, a_second], axis=1),
        ],
        axis=0,
    )
    docs = first, jnp.minimum(first + 1, DOCS - 1)
    return docs, ids, gates, b[:half, :], b[half:, :], right


def add_block(shape, block, me, acc, again, begin=0, end=None):
    experts, rank = shape
    half = rank // 2
    (first, second), ids, gates, even, odd, right = block
    end = experts + 1 if end is None else end
    left = []
    for e in range(begin, end):
        if e == experts:
            left.append(jnp.concatenate([even, odd], axis=1).astype(jnp.bfloat16))
            continue
        mine = (me * experts + e).astype(jnp.float32)
        w = jnp.sum(jnp.where(ids == mine, gates, 0.0), axis=0, keepdims=True)
        left.append(jnp.concatenate([w * even, w * odd], axis=1).astype(jnp.bfloat16))
    left = jnp.concatenate(left, axis=0)
    both = lax.dot_general(
        left, right, (((1,), (1,)), ((), ())), preferred_element_type=jnp.float32
    )
    rows = pl.ds(begin * half, (end - begin) * half)
    acc[first, rows, :] += both[:, : 2 * rank]
    again[second, rows, :] += both[:, 2 * rank :]


def origin_of(order, me, slot, tag, flip):
    origin = me ^ flip
    path = slot | tag
    for k in range(len(order[0])):
        hop = jnp.where((origin & 1) == 1, order[1][k], order[0][k])
        origin = origin ^ (((path >> k) & 1) * hop)
    return origin


def add_all(shape, order, blocks, height, offsets_ref, refs, acc, again):
    me = lax.axis_index("ctx").astype(jnp.int32)
    slots = refs[0].shape[0] // height

    def add(ref, s, base, tag, flip):
        source = origin_of(order, me, s, tag, flip)
        add_block(shape, prepare(shape, offsets_ref, ref, base, source), me, acc, again)

    if slots <= 4:
        for ref, (tag, flip) in zip(refs, blocks):
            for s in range(slots):
                add(ref, s, s * height, tag, flip)
        return

    def step(s, _):
        for ref, (tag, flip) in zip(refs, blocks):
            add(ref, s, pl.multiple_of(s * height, height), tag, flip)
        return 0

    lax.fori_loop(0, slots, step, 0)


def first_kernel(shape, order, blocks, height, offsets_ref, *refs):
    refs, (acc, again) = refs[:-2], refs[-2:]
    acc[...] = jnp.zeros_like(acc)
    again[...] = jnp.zeros_like(again)
    add_all(shape, order, blocks, height, offsets_ref, refs, acc, again)


def next_kernel(shape, order, blocks, height, offsets_ref, acc_in, again_in, *refs):
    add_all(shape, order, blocks, height, offsets_ref, refs[:-2], *refs[-2:])


def fold_kernel(shape, order, blocks, height, offsets_ref, acc_in, again, *refs):
    refs, acc = refs[:-1], refs[-1]
    add_all(shape, order, blocks, height, offsets_ref, refs, acc, again)
    acc[...] += again[...]


def last_kernel(shape, order, blocks, height, offsets_ref, held, *refs):
    experts, rank = shape
    half = rank // 2
    refs, (routed_hbm, shared_hbm, acc, shared_buf, sem) = refs[:-5], refs[-5:]
    me = lax.axis_index("ctx").astype(jnp.int32)
    slots = refs[0].shape[0] // height
    if slots <= 4:
        ready = [
            prepare(shape, offsets_ref, ref, s * height, origin_of(order, me, s, tag, flip))
            for ref, (tag, flip) in zip(refs, blocks)
            for s in range(slots)
        ]
    else:
        ready = []
        add_all(shape, order, blocks, height, offsets_ref, refs, acc, acc)
    rows = pl.ds(0, experts * half)
    copies = [
        pltpu.make_async_copy(acc.at[d, rows, :], routed_hbm.at[rows, d, :], sem.at[d])
        for d in range(DOCS)
    ]
    touched = [
        functools.reduce(jnp.logical_or, [doc == d for block in ready for doc in block[0]])
        if ready
        else True
        for d in range(DOCS)
    ]
    if ready:
        for copy, later in zip(copies, touched):
            pl.when(jnp.logical_not(later))(copy.start)
    for block in ready:
        add_block(shape, block, me, acc, acc)
    for copy, later in zip(copies, touched):
        if ready:
            pl.when(later)(copy.start)
        else:
            copy.start()
    columns = rank * rank * experts // EXPERTS
    place = experts * half + me * columns // 128
    for j in range(shared_buf.shape[1] // 128):
        for d in range(DOCS):
            shared_buf[d : d + 1, j * 128 : (j + 1) * 128] = acc[d, pl.ds(place + j, 1), :]
    copies.append(pltpu.make_async_copy(shared_buf, shared_hbm, sem.at[DOCS]))
    copies[-1].start()
    for copy in copies:
        copy.wait()


def on_device(devices, inputs, out_grads, gates, expert_ids, offsets, projections):
    tok, _ = inputs.shape
    rank = projections.shape[1] // 2
    half = rank // 2
    experts = EXPERTS // devices
    height, width = 16, tok * (2 * rank // 16) + tok + tok // 2
    smem = pl.BlockSpec(memory_space=pltpu.SMEM)
    vmem = pl.BlockSpec(memory_space=pltpu.VMEM)
    hbm = pl.BlockSpec(memory_space=pltpu.HBM)
    chunks = inputs.shape[1] // CHUNK
    params = pltpu.CompilerParams(vmem_limit_bytes=VMEM_LIMIT)

    def in_place(x):
        return pltpu.with_memory_space_constraint(x, pltpu.HBM)

    payload, offsets = pl.pallas_call(
        project_kernel,
        out_shape=(
            pltpu.VMEM((height, width), jnp.bfloat16),
            pltpu.SMEM(offsets.shape, jnp.int32),
        ),
        in_specs=[hbm] * 6,
        out_specs=(vmem, smem),
        scratch_shapes=[
            pltpu.VMEM((TOPK, tok), jnp.float32),
            pltpu.VMEM((TOPK, tok), jnp.int32),
            pltpu.VMEM(inputs.shape, jnp.bfloat16),
            pltpu.VMEM(inputs.shape, jnp.bfloat16),
            pltpu.VMEM(projections.shape, jnp.bfloat16),
            pltpu.VMEM((tok // 128, rank, 128), jnp.float32),
            pltpu.SemaphoreType.DMA((chunks,)),
            pltpu.SemaphoreType.DMA((chunks,)),
            pltpu.SemaphoreType.DMA((chunks,)),
            pltpu.SemaphoreType.DMA((3,)),
        ],
        compiler_params=params,
        name="project",
    )(*(in_place(x) for x in (gates.T, expert_ids.T, offsets, inputs, out_grads, projections)))

    far = [1 << k for k in range(devices.bit_length() - 2, 0, -1)]
    order = (far[:1] + far[-1:] + far[1:-1], far[1:-1] + far[:1] + far[-1:])
    last = len(far) - 1

    def swap(block, k):
        return lax.ppermute(block, "ctx", [(i, i ^ order[i & 1][k]) for i in range(devices)])

    def core(block):
        return lax.ppermute(block, "ctx", [(i, i ^ 1) for i in range(devices)])

    def after(block, acc):
        return lax.optimization_barrier((block, acc))

    shape = (experts, rank)
    rows = (experts + 1) * half
    sums = pltpu.VMEM((DOCS, rows, 2 * rank), jnp.float32)

    def add(name, blocks, acc=(), fold=False):
        kernel = fold_kernel if fold else next_kernel if acc else first_kernel
        return pl.pallas_call(
            functools.partial(kernel, shape, order, [b[1:] for b in blocks], height),
            out_shape=sums if fold else (sums, sums),
            in_specs=[smem] + [vmem] * (len(blocks) + len(acc)),
            out_specs=vmem if fold else (vmem, vmem),
            input_output_aliases={1: 0} if fold else {1: 0, 2: 1} if acc else {},
            compiler_params=params,
            name=name,
        )(offsets, *acc, *(b[0] for b in blocks))

    near = payload
    acc = add("sums_own", [(payload, 0, 0)])
    for k in range(last - 1):
        got = swap(near, k)
        if k == last - 2:
            early, acc = after(near, acc)
            two_early = swap(early, last)
        got, acc = after(got, acc)
        near = jnp.concatenate([near, got], axis=0)
        if k < last - 2:
            acc = add("sums_got", [(got, 1 << k, 0)], acc)
    bits = (1 << (last - 1), 1 << last)
    both = bits[0] | bits[1]
    one = swap(near, last - 1)
    acc = add("sums_got", [(got, 1 << (last - 2), 0)], acc)
    near, late, acc = lax.optimization_barrier((near, got, acc))
    two = jnp.concatenate([two_early, swap(late, last)], axis=0)
    near_core = core(near)
    one, acc = after(one, acc)
    three = swap(one, last)
    one_core = core(one)
    blocks = [(one, bits[0], 0), (two, bits[1], 0), (near_core, 0, 1), (one_core, bits[0], 1)]
    acc = add("sums_next", blocks, acc)
    two, acc = after(two, acc)
    two_core = core(two)
    three, acc = after(three, acc)
    three_core = core(three)
    acc = add("sums_three", [(three, both, 0), (two_core, bits[1], 1)], acc, fold=True)
    three_core, acc = after(three_core, acc)
    blocks = [(three_core, both, 1)]
    columns = rank * rank // devices
    routed, shared, _ = pl.pallas_call(
        functools.partial(last_kernel, shape, order, [b[1:] for b in blocks], height),
        out_shape=(
            jax.ShapeDtypeStruct((experts * half, DOCS, 2 * rank), jnp.float32),
            jax.ShapeDtypeStruct((DOCS, max(columns, 128)), jnp.float32),
            sums,
        ),
        in_specs=[smem] + [vmem] * (len(blocks) + 1),
        out_specs=(hbm, hbm, vmem),
        scratch_shapes=[
            pltpu.VMEM((DOCS, max(columns, 128)), jnp.float32),
            pltpu.SemaphoreType.DMA((DOCS + 1,)),
        ],
        input_output_aliases={1: 2},
        compiler_params=params,
        name="sums_last",
    )(offsets, acc, *(b[0] for b in blocks))
    routed = routed.reshape(experts, half, DOCS, 2 * rank).transpose(0, 2, 1, 3)
    routed = routed.reshape(experts, DOCS, rank * rank)
    if columns < 128:
        me = lax.axis_index("ctx")
        shared = lax.dynamic_slice_in_dim(shared, me * columns % 128, columns, 1)
    return shared, routed


def solution(mesh):
    placed = (
        P(("groups", "ctx"), None),
        P(("groups", "ctx"), None),
        P(("groups", "ctx"), None),
        P(("groups", "ctx"), None),
        P("groups"),
        P(),
    )
    return jax.shard_map(
        functools.partial(on_device, mesh.shape["ctx"]),
        mesh=mesh,
        in_specs=placed,
        out_specs=(P("groups", "ctx"), P("ctx", "groups", None)),
        check_vma=False,
    )
```

```python
import functools

import jax
import jax.numpy as jnp
from jax import lax
from jax.experimental import pallas as pl
from jax.experimental.pallas import tpu as pltpu
from jax.sharding import PartitionSpec as P

EXPERTS = 256
TOPK = 8
DOCS = 8
CHUNK = 3584
VMEM_LIMIT = 32 * 1024 * 1024


def doc_of(offsets_ref, start):
    doc = jnp.int32(0)
    for i in range(1, DOCS):
        doc = doc + (start >= offsets_ref[i]).astype(jnp.int32)
    return doc


def project_kernel(
    gates_hbm, ids_hbm, offsets_hbm, x_hbm, g_hbm, p_hbm, out_ref, offsets_ref,
    gates_ref, ids_ref, x_buf, g_buf, p_buf, rows_buf, x_sem, g_sem, p_sem, small_sem,
):
    tok, depth = x_hbm.shape
    rank = p_hbm.shape[1] // 2
    half = rank // 2
    chunks = depth // CHUNK
    small = (
        pltpu.make_async_copy(offsets_hbm, offsets_ref, small_sem.at[0]),
        pltpu.make_async_copy(gates_hbm, gates_ref, small_sem.at[1]),
        pltpu.make_async_copy(ids_hbm, ids_ref, small_sem.at[2]),
    )

    def copies(i):
        cols = pl.ds(i * CHUNK, CHUNK)
        return (
            pltpu.make_async_copy(p_hbm.at[cols, :], p_buf.at[cols, :], p_sem.at[i]),
            pltpu.make_async_copy(x_hbm.at[:, cols], x_buf.at[:, cols], x_sem.at[i]),
            pltpu.make_async_copy(g_hbm.at[:, cols], g_buf.at[:, cols], g_sem.at[i]),
        )

    for copy in copies(0) + small:
        copy.start()
    for i in range(1, chunks):
        for copy in copies(i):
            copy.start()
    for copy in small:
        copy.wait()
    gates = gates_ref[...]
    high = gates.astype(jnp.bfloat16).astype(jnp.float32)
    ids = ids_ref[...].astype(jnp.float32)
    base = 2 * rank // 16 * tok
    out_ref[:, base : base + tok] = jnp.concatenate([ids, high], axis=0).astype(jnp.bfloat16)
    low = gates - high
    out_ref[:, base + tok :] = jnp.concatenate(
        [low[:, : tok // 2], low[:, tok // 2 :]], axis=0
    ).astype(jnp.bfloat16)
    start = lax.axis_index("ctx").astype(jnp.int32) * tok
    first = doc_of(offsets_ref, start)
    second = jnp.minimum(first + 1, DOCS - 1)
    position = start + lax.broadcasted_iota(jnp.int32, (1, tok), 1)
    length = jnp.where(
        position < offsets_ref[first + 1],
        offsets_ref[first + 1] - offsets_ref[first],
        offsets_ref[second + 1] - offsets_ref[second],
    ).astype(jnp.float32)
    scale = lax.rsqrt(length)
    a = jnp.zeros((tok, rank), jnp.float32)
    b = jnp.zeros((tok, rank), jnp.float32)
    for i in range(chunks):
        for copy in copies(i)[:2]:
            copy.wait()
        cols = pl.ds(i * CHUNK, CHUNK)
        p = p_buf[cols, :]
        a = a + jnp.dot(x_buf[:, cols], p, preferred_element_type=jnp.float32)[:, :rank]
        copies(i)[2].wait()
        b = b + jnp.dot(g_buf[:, cols], p, preferred_element_type=jnp.float32)[:, rank:]
    both = jnp.concatenate([a, b], axis=1).T
    for k in range(rank // 16):
        rows = both[k * 16 : (k + 1) * 16, :]
        out_ref[:, k * tok : (k + 1) * tok] = rows.astype(jnp.bfloat16)
    scaled = both[rank:, :] * scale
    for j in range(tok // 128):
        lanes = slice(j * 128, (j + 1) * 128)
        rows_buf[j, :, :] = scaled[:, lanes]
        for odd in range(2):
            picked = rows_buf[j, pl.ds(odd, half, stride=2), :].astype(jnp.bfloat16)
            for k in range(half // 16):
                place = (rank + odd * half + k * 16) // 16 * tok + j * 128
                out_ref[:, place : place + 128] = picked[k * 16 : (k + 1) * 16, :]


def prepare(shape, offsets_ref, ref, base, source):
    rank = shape[1]
    half = rank // 2
    tok = 2 * ref.shape[1] // (4 * rank // 16 + 3)

    def rows(begin, count):
        parts = [
            ref[pl.ds(base, 16), k * tok : (k + 1) * tok]
            for k in range(begin // 16, (begin + count) // 16)
        ]
        return jnp.concatenate(parts, axis=0).astype(jnp.float32)

    start = source * tok
    first = doc_of(offsets_ref, start)
    position = start + lax.broadcasted_iota(jnp.int32, (1, tok), 1)
    in_first = (position < offsets_ref[first + 1]).astype(jnp.float32)
    a, b, named = rows(0, rank), rows(rank, rank), rows(2 * rank, 16)
    low = ref[pl.ds(base, 16), (2 * rank // 16 + 1) * tok :].astype(jnp.float32)
    low = jnp.concatenate([low[:8, :], low[8:, :]], axis=1)
    ids, gates = named[:8, :], (named[8:, :] + low) * (EXPERTS / TOPK) ** 0.5
    a_first = a * in_first
    a_second = (a - a_first).astype(jnp.bfloat16)
    a_first = a_first.astype(jnp.bfloat16)
    none = jnp.zeros_like(a_first)
    right = jnp.concatenate(
        [
            jnp.concatenate([a_first, none], axis=1),
            jnp.concatenate([none, a_first], axis=1),
            jnp.concatenate([a_second, none], axis=1),
            jnp.concatenate([none, a_second], axis=1),
        ],
        axis=0,
    )
    docs = first, jnp.minimum(first + 1, DOCS - 1)
    return docs, ids, gates, b[:half, :], b[half:, :], right


def add_block(shape, block, me, acc, again, begin=0, end=None):
    experts, rank = shape
    half = rank // 2
    (first, second), ids, gates, even, odd, right = block
    end = experts + 1 if end is None else end
    left = []
    for e in range(begin, end):
        if e == experts:
            left.append(jnp.concatenate([even, odd], axis=1).astype(jnp.bfloat16))
            continue
        mine = (me * experts + e).astype(jnp.float32)
        w = jnp.sum(jnp.where(ids == mine, gates, 0.0), axis=0, keepdims=True)
        left.append(jnp.concatenate([w * even, w * odd], axis=1).astype(jnp.bfloat16))
    left = jnp.concatenate(left, axis=0)
    both = lax.dot_general(
        left, right, (((1,), (1,)), ((), ())), preferred_element_type=jnp.float32
    )
    rows = pl.ds(begin * half, (end - begin) * half)
    acc[first, rows, :] += both[:, : 2 * rank]
    again[second, rows, :] += both[:, 2 * rank :]


def origin_of(order, me, slot, tag, flip):
    origin = me ^ flip
    path = slot | tag
    for k in range(len(order[0])):
        hop = jnp.where((origin & 1) == 1, order[1][k], order[0][k])
        origin = origin ^ (((path >> k) & 1) * hop)
    return origin


def add_all(shape, order, blocks, height, offsets_ref, refs, acc, again):
    me = lax.axis_index("ctx").astype(jnp.int32)
    def add(ref, s, base, tag, flip):
        source = origin_of(order, me, s, tag, flip)
        add_block(shape, prepare(shape, offsets_ref, ref, base, source), me, acc, again)

    for ref, (tag, flip) in zip(refs, blocks):
        slots = ref.shape[0] // height
        if slots <= 4:
            for s in range(slots):
                add(ref, s, s * height, tag, flip)
            continue

        def step(s, _, ref=ref, tag=tag, flip=flip):
            add(ref, s, pl.multiple_of(s * height, height), tag, flip)
            return 0

        lax.fori_loop(0, slots, step, 0)


def first_kernel(shape, order, blocks, height, offsets_ref, *refs):
    refs, (acc, again) = refs[:-2], refs[-2:]
    acc[...] = jnp.zeros_like(acc)
    again[...] = jnp.zeros_like(again)
    add_all(shape, order, blocks, height, offsets_ref, refs, acc, again)


def next_kernel(shape, order, blocks, height, offsets_ref, acc_in, again_in, *refs):
    add_all(shape, order, blocks, height, offsets_ref, refs[:-2], *refs[-2:])


def fold_kernel(shape, order, blocks, height, offsets_ref, acc_in, again, *refs):
    refs, acc = refs[:-1], refs[-1]
    add_all(shape, order, blocks, height, offsets_ref, refs, acc, again)
    acc[...] += again[...]


def last_kernel(shape, order, blocks, height, offsets_ref, held, *refs):
    experts, rank = shape
    half = rank // 2
    refs, (routed_hbm, shared_hbm, acc, shared_buf, sem) = refs[:-5], refs[-5:]
    me = lax.axis_index("ctx").astype(jnp.int32)
    slots = refs[0].shape[0] // height
    if slots <= 4:
        ready = [
            prepare(shape, offsets_ref, ref, s * height, origin_of(order, me, s, tag, flip))
            for ref, (tag, flip) in zip(refs, blocks)
            for s in range(slots)
        ]
    else:
        ready = []
        add_all(shape, order, blocks, height, offsets_ref, refs, acc, acc)
    rows = pl.ds(0, experts * half)
    copies = [
        pltpu.make_async_copy(acc.at[d, rows, :], routed_hbm.at[rows, d, :], sem.at[d])
        for d in range(DOCS)
    ]
    touched = [
        functools.reduce(jnp.logical_or, [doc == d for block in ready for doc in block[0]])
        if ready
        else True
        for d in range(DOCS)
    ]
    if ready:
        for copy, later in zip(copies, touched):
            pl.when(jnp.logical_not(later))(copy.start)
    for block in ready:
        add_block(shape, block, me, acc, acc)
    for copy, later in zip(copies, touched):
        if ready:
            pl.when(later)(copy.start)
        else:
            copy.start()
    columns = rank * rank * experts // EXPERTS
    place = experts * half + me * columns // 128
    for j in range(shared_buf.shape[1] // 128):
        for d in range(DOCS):
            shared_buf[d : d + 1, j * 128 : (j + 1) * 128] = acc[d, pl.ds(place + j, 1), :]
    copies.append(pltpu.make_async_copy(shared_buf, shared_hbm, sem.at[DOCS]))
    copies[-1].start()
    for copy in copies:
        copy.wait()


def on_device(devices, inputs, out_grads, gates, expert_ids, offsets, projections):
    tok, _ = inputs.shape
    rank = projections.shape[1] // 2
    half = rank // 2
    experts = EXPERTS // devices
    height, width = 16, tok * (2 * rank // 16) + tok + tok // 2
    smem = pl.BlockSpec(memory_space=pltpu.SMEM)
    vmem = pl.BlockSpec(memory_space=pltpu.VMEM)
    hbm = pl.BlockSpec(memory_space=pltpu.HBM)
    chunks = inputs.shape[1] // CHUNK
    params = pltpu.CompilerParams(vmem_limit_bytes=VMEM_LIMIT)

    def in_place(x):
        return pltpu.with_memory_space_constraint(x, pltpu.HBM)

    payload, offsets = pl.pallas_call(
        project_kernel,
        out_shape=(
            pltpu.VMEM((height, width), jnp.bfloat16),
            pltpu.SMEM(offsets.shape, jnp.int32),
        ),
        in_specs=[hbm] * 6,
        out_specs=(vmem, smem),
        scratch_shapes=[
            pltpu.VMEM((TOPK, tok), jnp.float32),
            pltpu.VMEM((TOPK, tok), jnp.int32),
            pltpu.VMEM(inputs.shape, jnp.bfloat16),
            pltpu.VMEM(inputs.shape, jnp.bfloat16),
            pltpu.VMEM(projections.shape, jnp.bfloat16),
            pltpu.VMEM((tok // 128, rank, 128), jnp.float32),
            pltpu.SemaphoreType.DMA((chunks,)),
            pltpu.SemaphoreType.DMA((chunks,)),
            pltpu.SemaphoreType.DMA((chunks,)),
            pltpu.SemaphoreType.DMA((3,)),
        ],
        compiler_params=params,
        name="project",
    )(*(in_place(x) for x in (gates.T, expert_ids.T, offsets, inputs, out_grads, projections)))

    far = [1 << k for k in range(devices.bit_length() - 2, 0, -1)]
    order = (far[:1] + far[-1:] + far[1:-1], far[1:-1] + far[:1] + far[-1:])
    last = len(far) - 1

    def swap(block, k):
        return lax.ppermute(block, "ctx", [(i, i ^ order[i & 1][k]) for i in range(devices)])

    def core(block):
        return lax.ppermute(block, "ctx", [(i, i ^ 1) for i in range(devices)])

    def after(block, acc):
        return lax.optimization_barrier((block, acc))

    shape = (experts, rank)
    rows = (experts + 1) * half
    sums = pltpu.VMEM((DOCS, rows, 2 * rank), jnp.float32)

    def add(name, blocks, acc=(), fold=False):
        kernel = fold_kernel if fold else next_kernel if acc else first_kernel
        return pl.pallas_call(
            functools.partial(kernel, shape, order, [b[1:] for b in blocks], height),
            out_shape=sums if fold else (sums, sums),
            in_specs=[smem] + [vmem] * (len(blocks) + len(acc)),
            out_specs=vmem if fold else (vmem, vmem),
            input_output_aliases={1: 0} if fold else {1: 0, 2: 1} if acc else {},
            compiler_params=params,
            name=name,
        )(offsets, *acc, *(b[0] for b in blocks))

    near = payload
    acc = add("sums_own", [(payload, 0, 0)])
    for k in range(last - 1):
        got = swap(near, k)
        if k == last - 2:
            early, acc = after(near, acc)
            two_early = swap(early, last)
        got, acc = after(got, acc)
        near = jnp.concatenate([near, got], axis=0)
        if k < last - 2:
            acc = add("sums_got", [(got, 1 << k, 0)], acc)
    bits = (1 << (last - 1), 1 << last)
    both = bits[0] | bits[1]
    one = swap(near, last - 1)
    acc = add("sums_got", [(got, 1 << (last - 2), 0)], acc)
    near, late, acc = lax.optimization_barrier((near, got, acc))
    two_late = swap(late, last)
    two = jnp.concatenate([two_early, two_late], axis=0)
    pair = jnp.concatenate([near, two_early], axis=0)
    pair_core = core(pair)
    near_core, early_core = pair_core[: near.shape[0]], pair_core[near.shape[0] :]
    one, acc = after(one, acc)
    three = swap(one, last)
    one_core = core(one)
    rest = bits[1] | 1 << (last - 2)
    blocks = [(one, bits[0], 0), (two, bits[1], 0)]
    blocks += [(near_core, 0, 1), (one_core, bits[0], 1), (early_core, bits[1], 1)]
    acc = add("sums_next", blocks, acc)
    two_late, acc = after(two_late, acc)
    late_core = core(two_late)
    three, late_core, acc = lax.optimization_barrier((three, late_core, acc))
    three_core = core(three)
    acc = add("sums_three", [(three, both, 0), (late_core, rest, 1)], acc, fold=True)
    three_core, acc = after(three_core, acc)
    blocks = [(three_core, both, 1)]
    columns = rank * rank // devices
    routed, shared, _ = pl.pallas_call(
        functools.partial(last_kernel, shape, order, [b[1:] for b in blocks], height),
        out_shape=(
            jax.ShapeDtypeStruct((experts * half, DOCS, 2 * rank), jnp.float32),
            jax.ShapeDtypeStruct((DOCS, max(columns, 128)), jnp.float32),
            sums,
        ),
        in_specs=[smem] + [vmem] * (len(blocks) + 1),
        out_specs=(hbm, hbm, vmem),
        scratch_shapes=[
            pltpu.VMEM((DOCS, max(columns, 128)), jnp.float32),
            pltpu.SemaphoreType.DMA((DOCS + 1,)),
        ],
        input_output_aliases={1: 2},
        compiler_params=params,
        name="sums_last",
    )(offsets, acc, *(b[0] for b in blocks))
    routed = routed.reshape(experts, half, DOCS, 2 * rank).transpose(0, 2, 1, 3)
    routed = routed.reshape(experts, DOCS, rank * rank)
    if columns < 128:
        me = lax.axis_index("ctx")
        shared = lax.dynamic_slice_in_dim(shared, me * columns % 128, columns, 1)
    return shared, routed


def solution(mesh):
    placed = (
        P(("groups", "ctx"), None),
        P(("groups", "ctx"), None),
        P(("groups", "ctx"), None),
        P(("groups", "ctx"), None),
        P("groups"),
        P(),
    )
    return jax.shard_map(
        functools.partial(on_device, mesh.shape["ctx"]),
        mesh=mesh,
        in_specs=placed,
        out_specs=(P("groups", "ctx"), P("ctx", "groups", None)),
        check_vma=False,
    )
```
